32 devices in a mesh: groups: 2 (over y), replica: 4 (over z), tensor: 4 (over x, core).
Axes of the slice: x: 2, y: 2, z: 4, core: 2. Of those that a mesh axis runs over, the one named last changes fastest.
Arguments:
- normed_hidden_rows: bfloat16 [24576, 8192], P(('groups', 'replica'), 'tensor'), parts along dimension 0, may hold values from -6 to 6
- block_adapter_index: int32 [192], P(('groups', 'replica')), parts along dimension 0, may hold values from 0 to 3
- transfer_plan: int32 [64, 2], P('groups'), parts along dimension 0, may hold values from -1 to 23, as said below
- key_value_weight: bfloat16 [8192, 2048], P('tensor'), may hold values from -0.0625 to 0.0625
- adapter_down_weight: bfloat16 [32, 64, 8192], P(('groups', 'replica'), None, 'tensor'), parts along dimension 0, may hold values from -0.0625 to 0.0625
- adapter_up_weight: bfloat16 [32, 64, 2048], P(('groups', 'replica'), None, 'tensor'), parts along dimension 0, may hold values from -0.75 to 0.75
Outputs:
- kv_out: bfloat16 [8192, 2048], P(('groups', 'replica'), 'tensor'), parts along dimension 0
The draws below stay inside these ranges and needn't reach their ends.
There are 2 independent parts, one for each index of `groups`. The reference program is written for one: setup_inputs(seed, part) draws one part's arguments, and reference() takes and returns one part's arrays. A program takes and returns all parts, laid end to end along the dimension named above; an argument that names none is the same for every part. Nothing has to cross between parts.
Inputs may be any that keep to these rules, and one draw needn't show every extreme that they name: `transfer_plan`: row d * 8 + j is slot j of replica d: column 0 a source replica, column 1 one of that replica's 24 blocks, both -1 in an empty slot. No block appears twice. One source fills at most 6 slots of one replica, and some source fills exactly 6 of some replica. Some replica has all 8 slots filled. Exactly one replica has all 24 of its blocks in the plan.
All inputs are finite; a program needn't handle non-finite values.
Results may differ from the reference program's by a relative error of at most 0.0029.
Values may be sent and summed in bfloat16 or wider, within the bound.
A program may use at most 128 MiB of HBM per device.

```python
import jax
import jax.numpy as jnp
from jax import lax

MODEL_WIDTH = 8192
ADAPTER_RANK = 64
BLOCK = 128
CAP = 8
ADAPTERS = 4
HOME = 24
KEY_VALUE_COLS = 2048
ROWS = 12288
ADAPTER_COUNT = 16
N_REPLICA = 4


def draw_transfer_plan(key, part):
    key = jax.random.fold_in(key, 7)
    subkeys = jax.random.split(key, 6)
    heavy = jax.random.randint(subkeys[0], (), 0, N_REPLICA)
    dest_shift = jax.random.randint(subkeys[1], (), 0, N_REPLICA)
    other_shift = jax.random.randint(subkeys[2], (), 0, N_REPLICA - 1)
    full_dest = jax.random.randint(subkeys[3], (), 0, N_REPLICA)
    dest_ids = jnp.arange(N_REPLICA, dtype=jnp.int32)[:, None]
    slot_ids = jnp.arange(CAP, dtype=jnp.int32)[None, :]
    slot_order = slot_ids * N_REPLICA + (dest_ids + dest_shift) % N_REPLICA
    is_heavy = slot_order < 3 * CAP
    other_source = (heavy + 1 + (dest_ids + slot_ids + other_shift) % (N_REPLICA - 1)) % N_REPLICA
    live_other = (jax.random.randint(subkeys[4], (N_REPLICA, CAP), 0, 4) > 0) | (dest_ids == full_dest)
    source = jnp.where(is_heavy, heavy, jnp.where(live_other, other_source, -1)).reshape(-1)
    onehot = (source[:, None] == jnp.arange(N_REPLICA, dtype=jnp.int32)[None, :]).astype(jnp.int32)
    before = jnp.cumsum(onehot, axis=0) - onehot
    source_rank = jnp.sum(before * onehot, axis=1)
    rotation = jax.random.randint(subkeys[5], (N_REPLICA,), 0, HOME)
    block_ids = jnp.where(source >= 0, (source_rank + rotation[jnp.maximum(source, 0)]) % HOME, -1)
    return jnp.stack([source, block_ids], axis=-1).astype(jnp.int32)


def touch_ends(result, key, smallest, largest):
    shape = result.shape
    place = [jax.random.randint(jax.random.fold_in(key, axis), (), 0, shape[axis]) for axis in range(len(shape))]
    result = result.at[tuple(place)].set(smallest)
    longest = shape.index(max(shape))
    place[longest] = (place[longest] + 1) % shape[longest]
    return result.at[tuple(place)].set(largest)


def levels(own_key, dims, cuts, smallest, top_value):
    factor_of, own = 1.0, jax.random.fold_in(own_key, 6)
    for dim, parts in cuts:
        draws = jnp.exp(jax.random.uniform(jax.random.fold_in(own, dim), (parts,), jnp.float32, smallest / len(cuts), top_value / len(cuts)))
        factor_of = factor_of * jnp.repeat(draws, dims[dim] // parts).reshape([-1 if axis == dim else 1 for axis in range(len(dims))])
    return factor_of


def noise(rng, shape, deviation, reach, pieces=(), held_as=jnp.bfloat16):
    values = jax.random.normal(rng, shape, jnp.float32) * deviation
    if len(pieces) > 0:
        values = levels(rng, shape, pieces, -0.22, 0.18) * values
    return jnp.clip(values, min=-reach, max=reach).astype(held_as)


def setup_inputs(seed: int = 0, part: int = 0) -> dict:
    key_list = jax.random.split(jax.random.key(seed), 7)
    part_splits = jax.random.split(jax.random.fold_in(key_list[6], part), 7)
    normed_hidden_rows = noise(part_splits[0], (ROWS, MODEL_WIDTH), 1.0, 6.0, ((0, 4), (1, 4)))
    block_adapter_index = touch_ends(jax.random.randint(part_splits[1], (N_REPLICA * HOME,), 0, ADAPTERS), jax.random.fold_in(part_splits[1], 1), 0, ADAPTERS - 1).astype(jnp.int32)
    transfer_plan = draw_transfer_plan(jax.random.fold_in(jax.random.fold_in(key_list[6], part), 71), part)
    key_value_weight = noise(key_list[3], (MODEL_WIDTH, KEY_VALUE_COLS), MODEL_WIDTH ** -0.5, 0.0625, ((0, 4),))
    adapter_down_weight = noise(part_splits[4], (ADAPTER_COUNT, ADAPTER_RANK, MODEL_WIDTH), MODEL_WIDTH ** -0.5, 0.0625, ((0, 4), (2, 4)))
    adapter_up_weight = noise(part_splits[5], (ADAPTER_COUNT, ADAPTER_RANK, KEY_VALUE_COLS), ADAPTER_RANK ** -0.5, 0.75, ((0, 4), (2, 4)))
    return {"normed_hidden_rows": normed_hidden_rows, "block_adapter_index": block_adapter_index, "transfer_plan": transfer_plan, "key_value_weight": key_value_weight, "adapter_down_weight": adapter_down_weight, "adapter_up_weight": adapter_up_weight}


adapter_scale = 0.5


def reference(normed_hidden_rows, block_adapter_index, transfer_plan, key_value_weight, adapter_down_weight, adapter_up_weight):
    blocks = normed_hidden_rows.reshape(N_REPLICA * HOME, BLOCK, MODEL_WIDTH)
    source = transfer_plan[:, 0]
    block_ids = transfer_plan[:, 1]
    is_live = source >= 0
    home_index = jnp.where(is_live, source * HOME + block_ids, 0).astype(jnp.int32)
    adapter = (jnp.maximum(source, 0) * ADAPTERS + block_adapter_index[home_index]).astype(jnp.int32)

    def project_slot(packed):
        index_home, adapter_index_lookup, rostered = packed
        token_rows = blocks[index_home]
        base_key_value = jnp.dot(token_rows, key_value_weight, preferred_element_type=jnp.float32)
        rank_reduced = jnp.dot(adapter_down_weight[adapter_index_lookup], token_rows.T, preferred_element_type=jnp.float32).astype(jnp.bfloat16)
        adapter_delta = jnp.dot(rank_reduced.T, adapter_up_weight[adapter_index_lookup], preferred_element_type=jnp.float32)
        projected_output = (base_key_value + adapter_scale * adapter_delta).astype(jnp.bfloat16)
        return jnp.where(rostered, projected_output, jnp.zeros_like(projected_output))

    projected = lax.map(project_slot, (home_index, adapter, is_live))
    return projected.reshape(N_REPLICA * CAP * BLOCK, KEY_VALUE_COLS)
```

```python
import functools

import jax
import jax.numpy as jnp
from jax import lax
from jax.experimental import pallas as pl
from jax.experimental.pallas import tpu as pltpu
from jax.sharding import PartitionSpec as P

adapter_scale = 0.5
PAIR = 2
KEEP = 4


def fused_kernel(
    sizes,
    plan_ref,
    adapter_ref,
    rows_hbm,
    weight_hbm,
    down_hbm,
    up_hbm,
    out_ref,
    rows,
    weight,
    down,
    down_t,
    up,
    lhs,
    send_a,
    recv_a,
    own,
    keep,
    send_b,
    recv_b,
    send_z,
    lanes,
    load_sem,
    up_send_sem,
    up_recv_sem,
    a_send_sem,
    a_recv_sem,
    b_send_sem,
    b_recv_sem,
    z_send_sem,
    z_recv_sem,
):
    replicas, cap, pair_cap, block, adapters, rank = sizes
    columns = out_ref.shape[1]
    step_rows = PAIR * block
    per_dest = pair_cap // PAIR
    remote_steps = (replicas - 1) * per_dest
    steps = replicas * per_dest

    me = lax.axis_index("replica")
    t = lax.axis_index("tensor")
    chip, core = t // 2, t % 2
    sibling = chip * 2 + (1 - core)
    across = (1 - chip) * 2 + core
    diagonal = (1 - chip) * 2 + (1 - core)
    roles = (diagonal, sibling, across, t)

    loads = []
    loads.append(pltpu.make_async_copy(up_hbm, up.at[3], load_sem.at[0]))
    loads.append(pltpu.make_async_copy(down_hbm, down, load_sem.at[1]))
    loads.append(pltpu.make_async_copy(rows_hbm, rows, load_sem.at[2]))
    for role in range(4):
        start = pl.multiple_of(roles[role] * columns, columns)
        loads.append(
            pltpu.make_async_copy(
                weight_hbm.at[:, pl.ds(start, columns)], weight.at[role], load_sem.at[3 + role]
            )
        )
    for load in loads:
        load.start()

    barrier = pltpu.get_barrier_semaphore()
    for peer in (sibling, across):
        pl.semaphore_signal(
            barrier, inc=1, device_id={"tensor": peer}, device_id_type=pl.DeviceIdType.MESH
        )
    for off in range(1, replicas):
        pl.semaphore_signal(
            barrier,
            inc=1,
            device_id={"replica": lax.rem(me + off, replicas)},
            device_id_type=pl.DeviceIdType.MESH,
        )
    pl.semaphore_wait(barrier, 2 + replicas - 1)

    def to_tensor(src, dst, send, recv, peer):
        return pltpu.make_async_remote_copy(
            src_ref=src,
            dst_ref=dst,
            send_sem=send,
            recv_sem=recv,
            device_id={"tensor": peer},
            device_id_type=pl.DeviceIdType.MESH,
        )

    loads[0].wait()
    up_across = to_tensor(up.at[3], up.at[2], up_send_sem.at[0], up_recv_sem.at[0], across)
    up_sibling = to_tensor(up.at[3], up.at[1], up_send_sem.at[1], up_recv_sem.at[1], sibling)
    up_forward = to_tensor(up.at[2], up.at[0], up_send_sem.at[2], up_recv_sem.at[2], sibling)
    up_across.start()
    up_sibling.start()
    loads[1].wait()
    down_t[...] = down[...].T
    up_across.wait_recv()
    up_forward.start()
    for load in loads[2:]:
        load.wait()
    up_sibling.wait_recv()
    up_forward.wait_recv()

    def copy_a(s):
        return to_tensor(
            send_a.at[lax.rem(s, 2)], recv_a.at[s], a_send_sem.at[lax.rem(s, 2)], a_recv_sem.at[s], sibling
        )

    def copy_b(s):
        return to_tensor(send_b.at[s], recv_b.at[s], b_send_sem.at[s], b_recv_sem.at[s], across)

    def offset_of(s):
        return 1 + lax.rem(s, replicas - 1), s // (replicas - 1)

    def copy_z(s):
        off, k = offset_of(s)
        return pltpu.make_async_remote_copy(
            src_ref=send_z.at[s],
            dst_ref=lanes.at[pl.ds(off * pair_cap + k * PAIR, PAIR)],
            send_sem=z_send_sem.at[s],
            recv_sem=z_recv_sem.at[s],
            device_id={"replica": lax.rem(me + off, replicas)},
            device_id_type=pl.DeviceIdType.MESH,
        )

    column_adapter = lax.broadcasted_iota(jnp.int32, (block, adapters * rank), 1) // rank

    def compute(s):
        off, k = offset_of(s)
        off = jnp.where(s < remote_steps, off, 0)
        k = jnp.where(s < remote_steps, k, s - remote_steps)
        dest = lax.rem(me + off, replicas)
        count = jnp.int32(0)
        picked = [jnp.int32(0)] * PAIR
        for j in range(cap):
            mine = plan_ref[dest * cap + j, 0] == me
            home = plan_ref[dest * cap + j, 1]
            for i in range(PAIR):
                picked[i] = jnp.where(mine & (count == k * PAIR + i), home, picked[i])
            count = count + jnp.where(mine, 1, 0)
        masks = []
        for i in range(PAIR):
            lhs[pl.ds(i * block, block), :] = rows[picked[i]]
            masks.append(column_adapter == adapter_ref[picked[i]])
        mask = jnp.concatenate(masks, axis=0)
        shrink = jnp.dot(lhs[...], down_t[...], preferred_element_type=jnp.float32)
        shrink = jnp.where(mask, shrink * adapter_scale, 0.0)
        high = shrink.astype(jnp.bfloat16)
        low = (shrink - high.astype(jnp.float32)).astype(jnp.bfloat16)

        def partial(role):
            return (
                jnp.dot(lhs[...], weight[role], preferred_element_type=jnp.float32)
                + jnp.dot(high, up[role], preferred_element_type=jnp.float32)
                + jnp.dot(low, up[role], preferred_element_type=jnp.float32)
            )

        slot = lax.rem(s, 2)

        @pl.when(s >= 2)
        def _():
            copy_a(s - 2).wait_send()

        send_a[slot, 0] = partial(0)
        send_a[slot, 1] = partial(1)
        copy_a(s).start()
        own[slot, 0] = partial(2)
        own[slot, 1] = partial(3)

    def stage_b(s):
        copy_a(s).wait_recv()
        slot = lax.rem(s, 2)
        send_b[s] = (own[slot, 0] + recv_a[s, 0]).astype(jnp.bfloat16)
        copy_b(s).start()
        keep[lax.rem(s, KEEP)] = own[slot, 1] + recv_a[s, 1]

    def stage_c(s):
        copy_b(s).wait_recv()
        total = keep[lax.rem(s, KEEP)] + recv_b[s].astype(jnp.float32)
        total = total.astype(jnp.bfloat16).reshape(PAIR, block, columns)

        @pl.when(s < remote_steps)
        def _():
            send_z[s] = total
            copy_z(s).start()

        @pl.when(s >= remote_steps)
        def _():
            lanes[pl.ds((s - remote_steps) * PAIR, PAIR)] = total

    def step(s, _):
        @pl.when(s < steps)
        def _():
            compute(s)

        @pl.when((s >= 1) & (s < steps + 1))
        def _():
            stage_b(s - 1)

        @pl.when(s >= KEEP)
        def _():
            stage_c(s - KEEP)

        return 0

    lax.fori_loop(0, steps + KEEP, step, 0)

    up_across.wait_send()
    up_sibling.wait_send()
    up_forward.wait_send()
    copy_a(steps - 2).wait_send()
    copy_a(steps - 1).wait_send()

    def drain_b(s, _):
        copy_b(s).wait_send()
        return 0

    lax.fori_loop(0, steps, drain_b, 0)

    def drain_z(s, _):
        copy_z(s).wait()
        return 0

    lax.fori_loop(0, remote_steps, drain_z, 0)

    count = [jnp.int32(0)] * replicas
    for j in range(cap):
        source = plan_ref[me * cap + j, 0]
        place = jnp.int32(0)
        for r in range(replicas):
            here = source == r
            place = jnp.where(here, lax.rem(me - r + replicas, replicas) * pair_cap + count[r], place)
            count[r] = count[r] + jnp.where(here, 1, 0)
        value = lanes[jnp.minimum(place, replicas * pair_cap - 1)]
        live = jnp.full(value.shape, source, jnp.int32) >= 0
        out_ref[pl.ds(j * block, block), :] = jnp.where(
            live, value.astype(jnp.float32), 0.0
        ).astype(jnp.bfloat16)


def fused(
    normed_hidden_rows,
    block_adapter_index,
    transfer_plan,
    key_value_weight,
    adapter_down_weight,
    adapter_up_weight,
    pair_cap,
):
    replicas = lax.axis_size("replica")
    cap = transfer_plan.shape[0] // replicas
    home = block_adapter_index.shape[0]
    width = normed_hidden_rows.shape[1]
    block = normed_hidden_rows.shape[0] // home
    adapters, rank, columns = adapter_up_weight.shape
    adapter_rows = adapters * rank
    steps = replicas * pair_cap // PAIR
    remote_steps = (replicas - 1) * pair_cap // PAIR
    step_rows = PAIR * block
    smem = pl.BlockSpec(memory_space=pltpu.SMEM)
    hbm = pl.BlockSpec(memory_space=pl.ANY)
    dma = pltpu.SemaphoreType.DMA
    sizes = (replicas, cap, pair_cap, block, adapters, rank)
    flops = 2 * steps * step_rows * width * 4 * columns
    return pl.pallas_call(
        functools.partial(fused_kernel, sizes),
        out_shape=jax.ShapeDtypeStruct((cap * block, columns), jnp.bfloat16),
        in_specs=[smem, smem, hbm, hbm, hbm, hbm],
        out_specs=pl.BlockSpec(memory_space=pltpu.VMEM),
        scratch_shapes=[
            pltpu.VMEM((home, block, width), jnp.bfloat16),
            pltpu.VMEM((4, width, columns), jnp.bfloat16),
            pltpu.VMEM((adapter_rows, width), jnp.bfloat16),
            pltpu.VMEM((width, adapter_rows), jnp.bfloat16),
            pltpu.VMEM((4, adapter_rows, columns), jnp.bfloat16),
            pltpu.VMEM((step_rows, width), jnp.bfloat16),
            pltpu.VMEM((2, 2, step_rows, columns), jnp.float32),
            pltpu.VMEM((steps, 2, step_rows, columns), jnp.float32),
            pltpu.VMEM((2, 2, step_rows, columns), jnp.float32),
            pltpu.VMEM((KEEP, step_rows, columns), jnp.float32),
            pltpu.VMEM((steps, step_rows, columns), jnp.bfloat16),
            pltpu.VMEM((steps, step_rows, columns), jnp.bfloat16),
            pltpu.VMEM((remote_steps, PAIR, block, columns), jnp.bfloat16),
            pltpu.VMEM((replicas * pair_cap, block, columns), jnp.bfloat16),
            dma((7,)),
            dma((3,)),
            dma((3,)),
            dma((2,)),
            dma((steps,)),
            dma((steps,)),
            dma((steps,)),
            dma((remote_steps,)),
            dma((remote_steps,)),
        ],
        compiler_params=pltpu.CompilerParams(
            collective_id=0, has_side_effects=True, vmem_limit_bytes=62 * 1024 * 1024
        ),
        cost_estimate=pl.CostEstimate(
            flops=flops, bytes_accessed=2 * normed_hidden_rows.size, transcendentals=0
        ),
    )(
        transfer_plan,
        block_adapter_index,
        normed_hidden_rows.reshape(home, block, width),
        key_value_weight,
        adapter_down_weight.reshape(adapter_rows, width),
        adapter_up_weight.reshape(adapter_rows, columns),
    )


def shards(
    normed_hidden_rows,
    block_adapter_index,
    transfer_plan,
    key_value_weight,
    adapter_down_weight,
    adapter_up_weight,
):
    replicas = lax.axis_size("replica")
    myself = lax.axis_index("replica")
    replica_slot_count = transfer_plan.shape[0] // replicas
    pair_cap = (3 * replica_slot_count + replicas - 1) // replicas
    if replicas == 4 and lax.axis_size("tensor") == 4 and pair_cap % PAIR == 0:
        return fused(
            normed_hidden_rows,
            block_adapter_index,
            transfer_plan,
            key_value_weight,
            adapter_down_weight,
            adapter_up_weight,
            pair_cap,
        )
    home_count = block_adapter_index.shape[0]
    queued_block_rows = normed_hidden_rows.shape[0] // home_count
    width_dev = normed_hidden_rows.shape[1]
    home_rows = normed_hidden_rows.reshape(home_count, queued_block_rows, width_dev)
    source = transfer_plan[:, 0].reshape(replicas, replica_slot_count)
    block_of = transfer_plan[:, 1].reshape(replicas, replica_slot_count)
    slot_ids = jnp.arange(replica_slot_count)
    earlier = slot_ids[None, :, None] > slot_ids[None, None, :]
    same_source = source[:, :, None] == source[:, None, :]
    order_rank = jnp.sum(same_source & earlier, axis=2)
    lane_ids = jnp.arange(pair_cap)
    outgoing = (source == myself)[:, None, :] & (order_rank[:, None, :] == lane_ids[None, :, None])
    sent_block = jnp.sum(jnp.where(outgoing, block_of[:, None, :], 0), axis=2).reshape(-1)
    sent_live = jnp.any(outgoing, axis=2).reshape(-1)
    home_ids = jnp.arange(home_count)
    pick_home = (sent_live[:, None] & (sent_block[:, None] == home_ids[None, :])).astype(
        jnp.bfloat16
    )
    replica_adapter = (
        block_adapter_index[:, None] == jnp.arange(adapter_down_weight.shape[0])[None, :]
    ).astype(jnp.bfloat16)
    forward_adapter = jnp.dot(
        pick_home, replica_adapter, preferred_element_type=jnp.float32
    ).astype(jnp.bfloat16)
    slots_out = replicas * pair_cap
    source_mine = lax.dynamic_index_in_dim(source, myself, 0, keepdims=False)
    rank_mine = lax.dynamic_index_in_dim(order_rank, myself, 0, keepdims=False)
    replica_ids = jnp.arange(replicas)
    incoming = (source_mine[:, None, None] == replica_ids[None, :, None]) & (
        rank_mine[:, None, None] == lane_ids[None, None, :]
    )
    incoming = incoming.reshape(replica_slot_count, slots_out).astype(jnp.bfloat16)

    def settle(received):
        flat = received.reshape((slots_out,) + received.shape[2:])
        return jnp.einsum("jp,pxy->jxy", incoming, flat, preferred_element_type=jnp.float32).astype(
            jnp.bfloat16
        )

    def lanes(sent):
        return sent.reshape((replicas, pair_cap) + sent.shape[1:])

    send_rows = jnp.einsum(
        "ph,hrc->prc", pick_home, home_rows, preferred_element_type=jnp.float32
    ).astype(jnp.bfloat16)
    send_up = jnp.einsum(
        "bi,ivx->bvx", forward_adapter, adapter_up_weight, preferred_element_type=jnp.float32
    ).astype(jnp.bfloat16)
    send_down = jnp.einsum(
        "rf,fwh->rwh", forward_adapter, adapter_down_weight, preferred_element_type=jnp.float32
    ).astype(jnp.bfloat16)
    got_rows, got_down, got_up = (
        lax.all_to_all(lanes(send_rows), "replica", split_axis=0, concat_axis=0, tiled=True),
        lax.all_to_all(lanes(send_down), "replica", split_axis=0, concat_axis=0, tiled=True),
        lax.all_to_all(lanes(send_up), "replica", split_axis=0, concat_axis=0, tiled=True),
    )
    block_rows = settle(got_rows)
    local_down = settle(got_down)
    up_slices = settle(got_up)
    partial_value = jnp.einsum(
        "jkd,jrd->jkr", local_down, block_rows, preferred_element_type=jnp.float32
    )
    rank_reduced = lax.psum(partial_value, "tensor").astype(jnp.bfloat16)
    block_count = block_rows.shape[0]
    base_terms = jnp.dot(
        block_rows.reshape(block_count * queued_block_rows, width_dev),
        key_value_weight,
        preferred_element_type=jnp.float32,
    )
    base_key_value = lax.psum_scatter(base_terms, "tensor", scatter_dimension=1, tiled=True)
    output_columns = base_key_value.shape[1]
    adapter_delta = jnp.einsum(
        "abq,abp->aqp", rank_reduced, up_slices, preferred_element_type=jnp.float32
    )
    projected_output = (
        base_key_value.reshape(block_count, queued_block_rows, output_columns)
        + adapter_scale * adapter_delta
    ).astype(jnp.bfloat16)
    return projected_output.reshape(replica_slot_count * queued_block_rows, output_columns)


def solution(mesh):
    return jax.shard_map(
        shards,
        mesh=mesh,
        in_specs=(
            P(("groups", "replica"), "tensor"),
            P(("groups", "replica")),
            P("groups", None),
            P("tensor", None),
            P(("groups", "replica"), None, "tensor"),
            P(("groups", "replica"), None, "tensor"),
        ),
        out_specs=P(("groups", "replica"), "tensor"),
        check_vma=False,
    )
```

```python
import functools

import jax
import jax.numpy as jnp
from jax import lax
from jax.experimental import pallas as pl
from jax.experimental.pallas import tpu as pltpu
from jax.sharding import PartitionSpec as P

adapter_scale = 0.5
PAIR = 2
KEEP = 4


def fused_kernel(
    sizes,
    plan_ref,
    adapter_ref,
    rows_hbm,
    weight_hbm,
    down_hbm,
    up_hbm,
    out_ref,
    rows,
    weight,
    down,
    down_t,
    up,
    lhs,
    send_a,
    recv_a,
    own,
    keep,
    send_b,
    recv_b,
    send_z,
    lanes,
    relay,
    load_sem,
    up_send_sem,
    up_recv_sem,
    a_send_sem,
    a_recv_sem,
    b_send_sem,
    b_recv_sem,
    z_send_sem,
    z_recv_sem,
    relay_sem,
):
    replicas, cap, pair_cap, block, adapters, rank = sizes
    columns = out_ref.shape[1]
    step_rows = PAIR * block
    per_dest = pair_cap // PAIR
    remote_steps = (replicas - 1) * per_dest
    steps = replicas * per_dest

    me = lax.axis_index("replica")
    t = lax.axis_index("tensor")
    chip, core = t // 2, t % 2
    sibling = chip * 2 + (1 - core)
    across = (1 - chip) * 2 + core
    diagonal = (1 - chip) * 2 + (1 - core)
    roles = (diagonal, sibling, across, t)

    loads = []
    loads.append(pltpu.make_async_copy(up_hbm, up.at[3], load_sem.at[0]))
    loads.append(pltpu.make_async_copy(down_hbm, down, load_sem.at[1]))
    loads.append(pltpu.make_async_copy(rows_hbm, rows, load_sem.at[2]))
    for role in range(4):
        start = pl.multiple_of(roles[role] * columns, columns)
        loads.append(
            pltpu.make_async_copy(
                weight_hbm.at[:, pl.ds(start, columns)], weight.at[role], load_sem.at[3 + role]
            )
        )
    for load in loads:
        load.start()

    barrier = pltpu.get_barrier_semaphore()
    for peer in (sibling, across):
        pl.semaphore_signal(
            barrier, inc=1, device_id={"tensor": peer}, device_id_type=pl.DeviceIdType.MESH
        )
    for off in range(1, replicas):
        pl.semaphore_signal(
            barrier,
            inc=1,
            device_id={"replica": lax.rem(me + off, replicas)},
            device_id_type=pl.DeviceIdType.MESH,
        )
    pl.semaphore_wait(barrier, 2 + replicas - 1)

    def to_tensor(src, dst, send, recv, peer):
        return pltpu.make_async_remote_copy(
            src_ref=src,
            dst_ref=dst,
            send_sem=send,
            recv_sem=recv,
            device_id={"tensor": peer},
            device_id_type=pl.DeviceIdType.MESH,
        )

    loads[0].wait()
    up_across = to_tensor(up.at[3], up.at[2], up_send_sem.at[0], up_recv_sem.at[0], across)
    up_sibling = to_tensor(up.at[3], up.at[1], up_send_sem.at[1], up_recv_sem.at[1], sibling)
    up_forward = to_tensor(up.at[2], up.at[0], up_send_sem.at[2], up_recv_sem.at[2], sibling)
    up_across.start()
    up_sibling.start()
    loads[1].wait()
    down_t[...] = down[...].T
    up_across.wait_recv()
    up_forward.start()
    for load in loads[2:]:
        load.wait()
    up_sibling.wait_recv()
    up_forward.wait_recv()

    def copy_a(s):
        return to_tensor(
            send_a.at[lax.rem(s, 2)], recv_a.at[s], a_send_sem.at[lax.rem(s, 2)], a_recv_sem.at[s], sibling
        )

    def copy_b(s):
        return to_tensor(send_b.at[s], recv_b.at[s], b_send_sem.at[s], b_recv_sem.at[s], across)

    half = me // 2
    partner = me + 1 - 2 * (me % 2)
    inner = (me == 1) | (me == 2)

    def place_of(s):
        c = s % 3
        dest = jnp.where(c < 2, (1 - half) * 2 + c, partner)
        return jnp.where(s < remote_steps, dest, me), jnp.where(
            s < remote_steps, s // 3, s - remote_steps
        )

    def relayed(s):
        return (s >= 3) & (s < remote_steps) & (s % 3 < 2)

    def lanes_of(source, k):
        return lanes.at[pl.ds(source * pair_cap + k * PAIR, PAIR)]

    def to_replica(src, dst, send, recv, peer):
        return pltpu.make_async_remote_copy(
            src_ref=src,
            dst_ref=dst,
            send_sem=send,
            recv_sem=recv,
            device_id={"replica": peer},
            device_id_type=pl.DeviceIdType.MESH,
        )

    def copy_z(s):
        dest, k = place_of(s)
        return to_replica(
            send_z.at[s], lanes_of(me, k), z_send_sem.at[s], z_recv_sem.at[me * per_dest + k], dest
        )

    def copy_relay(s):
        return to_replica(send_z.at[s], relay.at[s], z_send_sem.at[s], relay_sem.at[s], partner)

    def lane_of(s, i):
        dest, k = place_of(s)
        count = jnp.int32(0)
        home = jnp.int32(0)
        live = jnp.int32(0)
        for j in range(cap):
            mine = plan_ref[dest * cap + j, 0] == me
            here = mine & (count == k * PAIR + i)
            home = jnp.where(here, plan_ref[dest * cap + j, 1], home)
            live = jnp.where(here, 1, live)
            count = count + jnp.where(mine, 1, 0)
        return home, live

    column_adapter = lax.broadcasted_iota(jnp.int32, (block, adapters * rank), 1) // rank

    def compute(s):
        picked = [lane_of(s, i)[0] for i in range(PAIR)]
        masks = []
        for i in range(PAIR):
            lhs[pl.ds(i * block, block), :] = rows[picked[i]]
            masks.append(column_adapter == adapter_ref[picked[i]])
        mask = jnp.concatenate(masks, axis=0)
        shrink = jnp.dot(lhs[...], down_t[...], preferred_element_type=jnp.float32)
        shrink = jnp.where(mask, shrink * adapter_scale, 0.0)
        high = shrink.astype(jnp.bfloat16)
        low = (shrink - high.astype(jnp.float32)).astype(jnp.bfloat16)

        def partial(role):
            return (
                jnp.dot(lhs[...], weight[role], preferred_element_type=jnp.float32)
                + jnp.dot(high, up[role], preferred_element_type=jnp.float32)
                + jnp.dot(low, up[role], preferred_element_type=jnp.float32)
            )

        slot = lax.rem(s, 2)

        @pl.when(s >= 2)
        def _():
            copy_a(s - 2).wait_send()

        send_a[slot, 0] = partial(0)
        send_a[slot, 1] = partial(1)
        copy_a(s).start()
        own[slot, 0] = partial(2)
        own[slot, 1] = partial(3)

    def stage_b(s):
        copy_a(s).wait_recv()
        slot = lax.rem(s, 2)
        send_b[s] = (own[slot, 0] + recv_a[s, 0]).astype(jnp.bfloat16)
        copy_b(s).start()
        keep[lax.rem(s, KEEP)] = own[slot, 1] + recv_a[s, 1]

    def stage_c(s):
        copy_b(s).wait_recv()
        total = keep[lax.rem(s, KEEP)] + recv_b[s].astype(jnp.float32)
        total = total.astype(jnp.bfloat16).reshape(PAIR, block, columns)

        @pl.when(s < remote_steps)
        def _():
            send_z[s] = total

        @pl.when((s < remote_steps) & jnp.logical_not(relayed(s)))
        def _():
            copy_z(s).start()

        @pl.when(relayed(s) & jnp.logical_not(inner))
        def _():
            copy_relay(s).start()

        @pl.when(s >= remote_steps)
        def _():
            lanes[pl.ds(me * pair_cap + (s - remote_steps) * PAIR, PAIR)] = total

    def stage_d(s):
        @pl.when(relayed(s) & inner)
        def _():
            copy_relay(s).wait_recv()
            for i in range(PAIR):
                value = send_z[s, i].astype(jnp.float32)
                live = jnp.full(value.shape, lane_of(s, i)[1], jnp.int32) > 0
                other = relay[s, i].astype(jnp.float32)
                send_z[s, i] = jnp.where(live, value, other).astype(jnp.bfloat16)
            copy_z(s).start()

    def step(s, _):
        @pl.when(s < steps)
        def _():
            compute(s)

        @pl.when((s >= 1) & (s < steps + 1))
        def _():
            stage_b(s - 1)

        @pl.when(s >= KEEP)
        def _():
            stage_c(s - KEEP)

        @pl.when(s >= KEEP + 2)
        def _():
            stage_d(s - KEEP - 2)

        return 0

    lax.fori_loop(0, steps + KEEP, step, 0)

    up_across.wait_send()
    up_sibling.wait_send()
    up_forward.wait_send()
    copy_a(steps - 2).wait_send()
    copy_a(steps - 1).wait_send()

    def drain_b(s, _):
        copy_b(s).wait_send()
        return 0

    lax.fori_loop(0, steps, drain_b, 0)

    def drain_z(s, _):
        copy_z(s).wait_send()
        return 0

    lax.fori_loop(0, remote_steps, drain_z, 0)

    def arrived(source, k):
        to_replica(
            send_z.at[0], lanes_of(source, k), z_send_sem.at[0], z_recv_sem.at[source * per_dest + k], partner
        ).wait_recv()

    far_inner = jnp.where(half == 0, 2, 1)
    far_end = jnp.where(half == 0, 3, 0)
    for k in range(per_dest):
        arrived(partner, k)
        arrived(far_inner, k)
    arrived(far_end, 0)

    count = [jnp.int32(0)] * replicas
    for j in range(cap):
        source = plan_ref[me * cap + j, 0]
        place = jnp.int32(0)
        for r in range(replicas):
            here = source == r
            direct = r * pair_cap + count[r]
            if r in (0, 3):
                through = (1 if r == 0 else 2) * pair_cap + count[r]
                by_relay = (half != r // 2) & (count[r] >= PAIR)
                direct = jnp.where(by_relay, through, direct)
            place = jnp.where(here, direct, place)
            count[r] = count[r] + jnp.where(here, 1, 0)
        value = lanes[jnp.minimum(place, replicas * pair_cap - 1)]
        live = jnp.full(value.shape, source, jnp.int32) >= 0
        out_ref[pl.ds(j * block, block), :] = jnp.where(
            live, value.astype(jnp.float32), 0.0
        ).astype(jnp.bfloat16)


def fused(
    normed_hidden_rows,
    block_adapter_index,
    transfer_plan,
    key_value_weight,
    adapter_down_weight,
    adapter_up_weight,
    pair_cap,
):
    replicas = lax.axis_size("replica")
    cap = transfer_plan.shape[0] // replicas
    home = block_adapter_index.shape[0]
    width = normed_hidden_rows.shape[1]
    block = normed_hidden_rows.shape[0] // home
    adapters, rank, columns = adapter_up_weight.shape
    adapter_rows = adapters * rank
    steps = replicas * pair_cap // PAIR
    remote_steps = (replicas - 1) * pair_cap // PAIR
    step_rows = PAIR * block
    smem = pl.BlockSpec(memory_space=pltpu.SMEM)
    hbm = pl.BlockSpec(memory_space=pl.ANY)
    dma = pltpu.SemaphoreType.DMA
    sizes = (replicas, cap, pair_cap, block, adapters, rank)
    flops = 2 * steps * step_rows * width * 4 * columns
    return pl.pallas_call(
        functools.partial(fused_kernel, sizes),
        out_shape=jax.ShapeDtypeStruct((cap * block, columns), jnp.bfloat16),
        in_specs=[smem, smem, hbm, hbm, hbm, hbm],
        out_specs=pl.BlockSpec(memory_space=pltpu.VMEM),
        scratch_shapes=[
            pltpu.VMEM((home, block, width), jnp.bfloat16),
            pltpu.VMEM((4, width, columns), jnp.bfloat16),
            pltpu.VMEM((adapter_rows, width), jnp.bfloat16),
            pltpu.VMEM((width, adapter_rows), jnp.bfloat16),
            pltpu.VMEM((4, adapter_rows, columns), jnp.bfloat16),
            pltpu.VMEM((step_rows, width), jnp.bfloat16),
            pltpu.VMEM((2, 2, step_rows, columns), jnp.float32),
            pltpu.VMEM((steps, 2, step_rows, columns), jnp.float32),
            pltpu.VMEM((2, 2, step_rows, columns), jnp.float32),
            pltpu.VMEM((KEEP, step_rows, columns), jnp.float32),
            pltpu.VMEM((steps, step_rows, columns), jnp.bfloat16),
            pltpu.VMEM((steps, step_rows, columns), jnp.bfloat16),
            pltpu.VMEM((remote_steps, PAIR, block, columns), jnp.bfloat16),
            pltpu.VMEM((replicas * pair_cap, block, columns), jnp.bfloat16),
            pltpu.VMEM((remote_steps, PAIR, block, columns), jnp.bfloat16),
            dma((7,)),
            dma((3,)),
            dma((3,)),
            dma((2,)),
            dma((steps,)),
            dma((steps,)),
            dma((steps,)),
            dma((remote_steps,)),
            dma((steps,)),
            dma((remote_steps,)),
        ],
        compiler_params=pltpu.CompilerParams(
            collective_id=0, has_side_effects=True, vmem_limit_bytes=62 * 1024 * 1024
        ),
        cost_estimate=pl.CostEstimate(
            flops=flops, bytes_accessed=2 * normed_hidden_rows.size, transcendentals=0
        ),
    )(
        transfer_plan,
        block_adapter_index,
        normed_hidden_rows.reshape(home, block, width),
        key_value_weight,
        adapter_down_weight.reshape(adapter_rows, width),
        adapter_up_weight.reshape(adapter_rows, columns),
    )


def shards(
    normed_hidden_rows,
    block_adapter_index,
    transfer_plan,
    key_value_weight,
    adapter_down_weight,
    adapter_up_weight,
):
    replicas = lax.axis_size("replica")
    myself = lax.axis_index("replica")
    replica_slot_count = transfer_plan.shape[0] // replicas
    pair_cap = (3 * replica_slot_count + replicas - 1) // replicas
    one_full_source = (
        block_adapter_index.shape[0] == replicas * pair_cap
        and replica_slot_count - pair_cap <= PAIR
    )
    if replicas == 4 and lax.axis_size("tensor") == 4 and pair_cap % PAIR == 0 and one_full_source:
        return fused(
            normed_hidden_rows,
            block_adapter_index,
            transfer_plan,
            key_value_weight,
            adapter_down_weight,
            adapter_up_weight,
            pair_cap,
        )
    home_count = block_adapter_index.shape[0]
    queued_block_rows = normed_hidden_rows.shape[0] // home_count
    width_dev = normed_hidden_rows.shape[1]
    home_rows = normed_hidden_rows.reshape(home_count, queued_block_rows, width_dev)
    source = transfer_plan[:, 0].reshape(replicas, replica_slot_count)
    block_of = transfer_plan[:, 1].reshape(replicas, replica_slot_count)
    slot_ids = jnp.arange(replica_slot_count)
    earlier = slot_ids[None, :, None] > slot_ids[None, None, :]
    same_source = source[:, :, None] == source[:, None, :]
    order_rank = jnp.sum(same_source & earlier, axis=2)
    lane_ids = jnp.arange(pair_cap)
    outgoing = (source == myself)[:, None, :] & (order_rank[:, None, :] == lane_ids[None, :, None])
    sent_block = jnp.sum(jnp.where(outgoing, block_of[:, None, :], 0), axis=2).reshape(-1)
    sent_live = jnp.any(outgoing, axis=2).reshape(-1)
    home_ids = jnp.arange(home_count)
    pick_home = (sent_live[:, None] & (sent_block[:, None] == home_ids[None, :])).astype(
        jnp.bfloat16
    )
    replica_adapter = (
        block_adapter_index[:, None] == jnp.arange(adapter_down_weight.shape[0])[None, :]
    ).astype(jnp.bfloat16)
    forward_adapter = jnp.dot(
        pick_home, replica_adapter, preferred_element_type=jnp.float32
    ).astype(jnp.bfloat16)
    slots_out = replicas * pair_cap
    source_mine = lax.dynamic_index_in_dim(source, myself, 0, keepdims=False)
    rank_mine = lax.dynamic_index_in_dim(order_rank, myself, 0, keepdims=False)
    replica_ids = jnp.arange(replicas)
    incoming = (source_mine[:, None, None] == replica_ids[None, :, None]) & (
        rank_mine[:, None, None] == lane_ids[None, None, :]
    )
    incoming = incoming.reshape(replica_slot_count, slots_out).astype(jnp.bfloat16)

    def settle(received):
        flat = received.reshape((slots_out,) + received.shape[2:])
        return jnp.einsum("jp,pxy->jxy", incoming, flat, preferred_element_type=jnp.float32).astype(
            jnp.bfloat16
        )

    def lanes(sent):
        return sent.reshape((replicas, pair_cap) + sent.shape[1:])

    send_rows = jnp.einsum(
        "ph,hrc->prc", pick_home, home_rows, preferred_element_type=jnp.float32
    ).astype(jnp.bfloat16)
    send_up = jnp.einsum(
        "bi,ivx->bvx", forward_adapter, adapter_up_weight, preferred_element_type=jnp.float32
    ).astype(jnp.bfloat16)
    send_down = jnp.einsum(
        "rf,fwh->rwh", forward_adapter, adapter_down_weight, preferred_element_type=jnp.float32
    ).astype(jnp.bfloat16)
    got_rows, got_down, got_up = (
        lax.all_to_all(lanes(send_rows), "replica", split_axis=0, concat_axis=0, tiled=True),
        lax.all_to_all(lanes(send_down), "replica", split_axis=0, concat_axis=0, tiled=True),
        lax.all_to_all(lanes(send_up), "replica", split_axis=0, concat_axis=0, tiled=True),
    )
    block_rows = settle(got_rows)
    local_down = settle(got_down)
    up_slices = settle(got_up)
    partial_value = jnp.einsum(
        "jkd,jrd->jkr", local_down, block_rows, preferred_element_type=jnp.float32
    )
    rank_reduced = lax.psum(partial_value, "tensor").astype(jnp.bfloat16)
    block_count = block_rows.shape[0]
    base_terms = jnp.dot(
        block_rows.reshape(block_count * queued_block_rows, width_dev),
        key_value_weight,
        preferred_element_type=jnp.float32,
    )
    base_key_value = lax.psum_scatter(base_terms, "tensor", scatter_dimension=1, tiled=True)
    output_columns = base_key_value.shape[1]
    adapter_delta = jnp.einsum(
        "abq,abp->aqp", rank_reduced, up_slices, preferred_element_type=jnp.float32
    )
    projected_output = (
        base_key_value.reshape(block_count, queued_block_rows, output_columns)
        + adapter_scale * adapter_delta
    ).astype(jnp.bfloat16)
    return projected_output.reshape(replica_slot_count * queued_block_rows, output_columns)


def solution(mesh):
    return jax.shard_map(
        shards,
        mesh=mesh,
        in_specs=(
            P(("groups", "replica"), "tensor"),
            P(("groups", "replica")),
            P("groups", None),
            P("tensor", None),
            P(("groups", "replica"), None, "tensor"),
            P(("groups", "replica"), None, "tensor"),
        ),
        out_specs=P(("groups", "replica"), "tensor"),
        check_vma=False,
    )
```

```python
import functools

import jax
import jax.numpy as jnp
from jax import lax
from jax.experimental import pallas as pl
from jax.experimental.pallas import tpu as pltpu
from jax.sharding import PartitionSpec as P

adapter_scale = 0.5
PAIR = 2
KEEP = 4


def fused_kernel(
    sizes,
    plan_ref,
    adapter_ref,
    rows_hbm,
    weight_hbm,
    down_hbm,
    up_hbm,
    out_ref,
    rows,
    weight,
    down,
    down_t,
    up,
    lhs,
    send_a,
    recv_a,
    own,
    keep,
    send_b,
    recv_b,
    send_z,
    lanes,
    relay,
    load_sem,
    up_send_sem,
    up_recv_sem,
    a_send_sem,
    a_recv_sem,
    b_send_sem,
    b_recv_sem,
    z_send_sem,
    z_recv_sem,
    relay_sem,
):
    replicas, cap, pair_cap, block, adapters, rank = sizes
    columns = out_ref.shape[1]
    step_rows = PAIR * block
    per_dest = pair_cap // PAIR
    remote_steps = (replicas - 1) * per_dest
    steps = replicas * per_dest

    me = lax.axis_index("replica")
    t = lax.axis_index("tensor")
    chip, core = t // 2, t % 2
    sibling = chip * 2 + (1 - core)
    across = (1 - chip) * 2 + core
    diagonal = (1 - chip) * 2 + (1 - core)
    roles = (diagonal, sibling, across, t)

    loads = []
    loads.append(pltpu.make_async_copy(up_hbm, up.at[3], load_sem.at[0]))
    loads.append(pltpu.make_async_copy(down_hbm, down, load_sem.at[1]))
    loads.append(pltpu.make_async_copy(rows_hbm, rows, load_sem.at[2]))
    for role in range(4):
        start = pl.multiple_of(roles[role] * columns, columns)
        loads.append(
            pltpu.make_async_copy(
                weight_hbm.at[:, pl.ds(start, columns)], weight.at[role], load_sem.at[3 + role]
            )
        )
    for load in loads:
        load.start()

    barrier = pltpu.get_barrier_semaphore()
    for peer in (sibling, across):
        pl.semaphore_signal(
            barrier, inc=1, device_id={"tensor": peer}, device_id_type=pl.DeviceIdType.MESH
        )
    for off in range(1, replicas):
        pl.semaphore_signal(
            barrier,
            inc=1,
            device_id={"replica": lax.rem(me + off, replicas)},
            device_id_type=pl.DeviceIdType.MESH,
        )
    pl.semaphore_wait(barrier, 2 + replicas - 1)

    def to_tensor(src, dst, send, recv, peer):
        return pltpu.make_async_remote_copy(
            src_ref=src,
            dst_ref=dst,
            send_sem=send,
            recv_sem=recv,
            device_id={"tensor": peer},
            device_id_type=pl.DeviceIdType.MESH,
        )

    loads[0].wait()
    up_across = to_tensor(up.at[3], up.at[2], up_send_sem.at[0], up_recv_sem.at[0], across)
    up_sibling = to_tensor(up.at[3], up.at[1], up_send_sem.at[1], up_recv_sem.at[1], sibling)
    up_forward = to_tensor(up.at[2], up.at[0], up_send_sem.at[2], up_recv_sem.at[2], sibling)
    up_across.start()
    up_sibling.start()
    loads[1].wait()
    down_t[...] = down[...].T
    up_across.wait_recv()
    up_forward.start()
    for load in loads[2:]:
        load.wait()
    up_sibling.wait_recv()
    up_forward.wait_recv()

    def copy_a(s):
        return to_tensor(
            send_a.at[lax.rem(s, 2)], recv_a.at[s], a_send_sem.at[lax.rem(s, 2)], a_recv_sem.at[s], sibling
        )

    def copy_b(s):
        return to_tensor(send_b.at[s], recv_b.at[s], b_send_sem.at[s], b_recv_sem.at[s], across)

    half = me // 2
    partner = me + 1 - 2 * (me % 2)
    inner = (me == 1) | (me == 2)

    def place_of(s):
        c = s % 3
        dest = jnp.where(c < 2, (1 - half) * 2 + c, partner)
        return jnp.where(s < remote_steps, dest, me), jnp.where(
            s < remote_steps, s // 3, s - remote_steps
        )

    def relayed(s):
        return (s >= 3) & (s < remote_steps) & (s % 3 < 2)

    def lanes_of(source, k):
        return lanes.at[pl.ds(source * pair_cap + k * PAIR, PAIR)]

    def to_replica(src, dst, send, recv, peer):
        return pltpu.make_async_remote_copy(
            src_ref=src,
            dst_ref=dst,
            send_sem=send,
            recv_sem=recv,
            device_id={"replica": peer},
            device_id_type=pl.DeviceIdType.MESH,
        )

    def copy_z(s):
        dest, k = place_of(s)
        return to_replica(
            send_z.at[s], lanes_of(me, k), z_send_sem.at[s], z_recv_sem.at[me * per_dest + k], dest
        )

    def copy_relay(s):
        return to_replica(send_z.at[s], relay.at[s], z_send_sem.at[s], relay_sem.at[s], partner)

    def lane_of(s, i):
        dest, k = place_of(s)
        count = jnp.int32(0)
        home = jnp.int32(0)
        live = jnp.int32(0)
        for j in range(cap):
            mine = plan_ref[dest * cap + j, 0] == me
            here = mine & (count == k * PAIR + i)
            home = jnp.where(here, plan_ref[dest * cap + j, 1], home)
            live = jnp.where(here, 1, live)
            count = count + jnp.where(mine, 1, 0)
        return home, live

    column_adapter = lax.broadcasted_iota(jnp.int32, (block, adapters * rank), 1) // rank

    def compute(s):
        picked = [lane_of(s, i)[0] for i in range(PAIR)]
        masks = []
        for i in range(PAIR):
            lhs[pl.ds(i * block, block), :] = rows[picked[i]]
            masks.append(column_adapter == adapter_ref[picked[i]])
        mask = jnp.concatenate(masks, axis=0)
        shrink = jnp.dot(lhs[...], down_t[...], preferred_element_type=jnp.float32)
        shrink = jnp.where(mask, shrink * adapter_scale, 0.0)
        high = shrink.astype(jnp.bfloat16)
        low = (shrink - high.astype(jnp.float32)).astype(jnp.bfloat16)

        def partial(role):
            return (
                jnp.dot(lhs[...], weight[role], preferred_element_type=jnp.float32)
                + jnp.dot(high, up[role], preferred_element_type=jnp.float32)
                + jnp.dot(low, up[role], preferred_element_type=jnp.float32)
            )

        slot = lax.rem(s, 2)

        @pl.when(s >= 2)
        def _():
            copy_a(s - 2).wait_send()

        send_a[slot, 0] = partial(0)
        send_a[slot, 1] = partial(1)
        copy_a(s).start()
        own[slot, 0] = partial(2)
        own[slot, 1] = partial(3)

    def stage_b(s):
        copy_a(s).wait_recv()
        slot = lax.rem(s, 2)
        send_b[s] = (own[slot, 0] + recv_a[s, 0]).astype(jnp.bfloat16)
        copy_b(s).start()
        keep[lax.rem(s, KEEP)] = own[slot, 1] + recv_a[s, 1]

    def stage_c(s):
        copy_b(s).wait_recv()
        total = keep[lax.rem(s, KEEP)] + recv_b[s].astype(jnp.float32)
        total = total.astype(jnp.bfloat16).reshape(PAIR, block, columns)

        @pl.when(s < remote_steps)
        def _():
            send_z[s] = total

        @pl.when((s < remote_steps) & jnp.logical_not(relayed(s)))
        def _():
            copy_z(s).start()

        @pl.when(relayed(s) & jnp.logical_not(inner))
        def _():
            copy_relay(s).start()

        @pl.when(s >= remote_steps)
        def _():
            lanes[pl.ds(me * pair_cap + (s - remote_steps) * PAIR, PAIR)] = total

    def stage_d(s):
        @pl.when(relayed(s) & inner)
        def _():
            copy_relay(s).wait_recv()
            for i in range(PAIR):
                value = send_z[s, i].astype(jnp.float32)
                live = jnp.full(value.shape, lane_of(s, i)[1], jnp.int32) > 0
                other = relay[s, i].astype(jnp.float32)
                send_z[s, i] = jnp.where(live, value, other).astype(jnp.bfloat16)
            copy_z(s).start()

    def step(s, _):
        @pl.when((s >= 1) & (s < steps + 1))
        def _():
            stage_b(s - 1)

        @pl.when(s >= KEEP)
        def _():
            stage_c(s - KEEP)

        @pl.when(s >= KEEP + 2)
        def _():
            stage_d(s - KEEP - 2)

        @pl.when(s < steps)
        def _():
            compute(s)

        return 0

    lax.fori_loop(0, steps + KEEP, step, 0)

    up_across.wait_send()
    up_sibling.wait_send()
    up_forward.wait_send()
    copy_a(steps - 2).wait_send()
    copy_a(steps - 1).wait_send()

    def drain_b(s, _):
        copy_b(s).wait_send()
        return 0

    lax.fori_loop(0, steps, drain_b, 0)

    def drain_z(s, _):
        copy_z(s).wait_send()
        return 0

    lax.fori_loop(0, remote_steps, drain_z, 0)

    def arrived(source, k):
        to_replica(
            send_z.at[0], lanes_of(source, k), z_send_sem.at[0], z_recv_sem.at[source * per_dest + k], partner
        ).wait_recv()

    far_inner = jnp.where(half == 0, 2, 1)
    far_end = jnp.where(half == 0, 3, 0)
    for k in range(per_dest):
        arrived(partner, k)
        arrived(far_inner, k)
    arrived(far_end, 0)

    count = [jnp.int32(0)] * replicas
    for j in range(cap):
        source = plan_ref[me * cap + j, 0]
        place = jnp.int32(0)
        for r in range(replicas):
            here = source == r
            direct = r * pair_cap + count[r]
            if r in (0, 3):
                through = (1 if r == 0 else 2) * pair_cap + count[r]
                by_relay = (half != r // 2) & (count[r] >= PAIR)
                direct = jnp.where(by_relay, through, direct)
            place = jnp.where(here, direct, place)
            count[r] = count[r] + jnp.where(here, 1, 0)
        value = lanes[jnp.minimum(place, replicas * pair_cap - 1)]
        live = jnp.full(value.shape, source, jnp.int32) >= 0
        out_ref[pl.ds(j * block, block), :] = jnp.where(
            live, value.astype(jnp.float32), 0.0
        ).astype(jnp.bfloat16)


def fused(
    normed_hidden_rows,
    block_adapter_index,
    transfer_plan,
    key_value_weight,
    adapter_down_weight,
    adapter_up_weight,
    pair_cap,
):
    replicas = lax.axis_size("replica")
    cap = transfer_plan.shape[0] // replicas
    home = block_adapter_index.shape[0]
    width = normed_hidden_rows.shape[1]
    block = normed_hidden_rows.shape[0] // home
    adapters, rank, columns = adapter_up_weight.shape
    adapter_rows = adapters * rank
    steps = replicas * pair_cap // PAIR
    remote_steps = (replicas - 1) * pair_cap // PAIR
    step_rows = PAIR * block
    smem = pl.BlockSpec(memory_space=pltpu.SMEM)
    hbm = pl.BlockSpec(memory_space=pl.ANY)
    dma = pltpu.SemaphoreType.DMA
    sizes = (replicas, cap, pair_cap, block, adapters, rank)
    flops = 2 * steps * step_rows * width * 4 * columns
    return pl.pallas_call(
        functools.partial(fused_kernel, sizes),
        out_shape=jax.ShapeDtypeStruct((cap * block, columns), jnp.bfloat16),
        in_specs=[smem, smem, hbm, hbm, hbm, hbm],
        out_specs=pl.BlockSpec(memory_space=pltpu.VMEM),
        scratch_shapes=[
            pltpu.VMEM((home, block, width), jnp.bfloat16),
            pltpu.VMEM((4, width, columns), jnp.bfloat16),
            pltpu.VMEM((adapter_rows, width), jnp.bfloat16),
            pltpu.VMEM((width, adapter_rows), jnp.bfloat16),
            pltpu.VMEM((4, adapter_rows, columns), jnp.bfloat16),
            pltpu.VMEM((step_rows, width), jnp.bfloat16),
            pltpu.VMEM((2, 2, step_rows, columns), jnp.float32),
            pltpu.VMEM((steps, 2, step_rows, columns), jnp.float32),
            pltpu.VMEM((2, 2, step_rows, columns), jnp.float32),
            pltpu.VMEM((KEEP, step_rows, columns), jnp.float32),
            pltpu.VMEM((steps, step_rows, columns), jnp.bfloat16),
            pltpu.VMEM((steps, step_rows, columns), jnp.bfloat16),
            pltpu.VMEM((remote_steps, PAIR, block, columns), jnp.bfloat16),
            pltpu.VMEM((replicas * pair_cap, block, columns), jnp.bfloat16),
            pltpu.VMEM((remote_steps, PAIR, block, columns), jnp.bfloat16),
            dma((7,)),
            dma((3,)),
            dma((3,)),
            dma((2,)),
            dma((steps,)),
            dma((steps,)),
            dma((steps,)),
            dma((remote_steps,)),
            dma((steps,)),
            dma((remote_steps,)),
        ],
        compiler_params=pltpu.CompilerParams(
            collective_id=0, has_side_effects=True, vmem_limit_bytes=62 * 1024 * 1024
        ),
        cost_estimate=pl.CostEstimate(
            flops=flops, bytes_accessed=2 * normed_hidden_rows.size, transcendentals=0
        ),
    )(
        transfer_plan,
        block_adapter_index,
        normed_hidden_rows.reshape(home, block, width),
        key_value_weight,
        adapter_down_weight.reshape(adapter_rows, width),
        adapter_up_weight.reshape(adapter_rows, columns),
    )


def shards(
    normed_hidden_rows,
    block_adapter_index,
    transfer_plan,
    key_value_weight,
    adapter_down_weight,
    adapter_up_weight,
):
    replicas = lax.axis_size("replica")
    myself = lax.axis_index("replica")
    replica_slot_count = transfer_plan.shape[0] // replicas
    pair_cap = (3 * replica_slot_count + replicas - 1) // replicas
    one_full_source = (
        block_adapter_index.shape[0] == replicas * pair_cap
        and replica_slot_count - pair_cap <= PAIR
    )
    if replicas == 4 and lax.axis_size("tensor") == 4 and pair_cap % PAIR == 0 and one_full_source:
        return fused(
            normed_hidden_rows,
            block_adapter_index,
            transfer_plan,
            key_value_weight,
            adapter_down_weight,
            adapter_up_weight,
            pair_cap,
        )
    home_count = block_adapter_index.shape[0]
    queued_block_rows = normed_hidden_rows.shape[0] // home_count
    width_dev = normed_hidden_rows.shape[1]
    home_rows = normed_hidden_rows.reshape(home_count, queued_block_rows, width_dev)
    source = transfer_plan[:, 0].reshape(replicas, replica_slot_count)
    block_of = transfer_plan[:, 1].reshape(replicas, replica_slot_count)
    slot_ids = jnp.arange(replica_slot_count)
    earlier = slot_ids[None, :, None] > slot_ids[None, None, :]
    same_source = source[:, :, None] == source[:, None, :]
    order_rank = jnp.sum(same_source & earlier, axis=2)
    lane_ids = jnp.arange(pair_cap)
    outgoing = (source == myself)[:, None, :] & (order_rank[:, None, :] == lane_ids[None, :, None])
    sent_block = jnp.sum(jnp.where(outgoing, block_of[:, None, :], 0), axis=2).reshape(-1)
    sent_live = jnp.any(outgoing, axis=2).reshape(-1)
    home_ids = jnp.arange(home_count)
    pick_home = (sent_live[:, None] & (sent_block[:, None] == home_ids[None, :])).astype(
        jnp.bfloat16
    )
    replica_adapter = (
        block_adapter_index[:, None] == jnp.arange(adapter_down_weight.shape[0])[None, :]
    ).astype(jnp.bfloat16)
    forward_adapter = jnp.dot(
        pick_home, replica_adapter, preferred_element_type=jnp.float32
    ).astype(jnp.bfloat16)
    slots_out = replicas * pair_cap
    source_mine = lax.dynamic_index_in_dim(source, myself, 0, keepdims=False)
    rank_mine = lax.dynamic_index_in_dim(order_rank, myself, 0, keepdims=False)
    replica_ids = jnp.arange(replicas)
    incoming = (source_mine[:, None, None] == replica_ids[None, :, None]) & (
        rank_mine[:, None, None] == lane_ids[None, None, :]
    )
    incoming = incoming.reshape(replica_slot_count, slots_out).astype(jnp.bfloat16)

    def settle(received):
        flat = received.reshape((slots_out,) + received.shape[2:])
        return jnp.einsum("jp,pxy->jxy", incoming, flat, preferred_element_type=jnp.float32).astype(
            jnp.bfloat16
        )

    def lanes(sent):
        return sent.reshape((replicas, pair_cap) + sent.shape[1:])

    send_rows = jnp.einsum(
        "ph,hrc->prc", pick_home, home_rows, preferred_element_type=jnp.float32
    ).astype(jnp.bfloat16)
    send_up = jnp.einsum(
        "bi,ivx->bvx", forward_adapter, adapter_up_weight, preferred_element_type=jnp.float32
    ).astype(jnp.bfloat16)
    send_down = jnp.einsum(
        "rf,fwh->rwh", forward_adapter, adapter_down_weight, preferred_element_type=jnp.float32
    ).astype(jnp.bfloat16)
    got_rows, got_down, got_up = (
        lax.all_to_all(lanes(send_rows), "replica", split_axis=0, concat_axis=0, tiled=True),
        lax.all_to_all(lanes(send_down), "replica", split_axis=0, concat_axis=0, tiled=True),
        lax.all_to_all(lanes(send_up), "replica", split_axis=0, concat_axis=0, tiled=True),
    )
    block_rows = settle(got_rows)
    local_down = settle(got_down)
    up_slices = settle(got_up)
    partial_value = jnp.einsum(
        "jkd,jrd->jkr", local_down, block_rows, preferred_element_type=jnp.float32
    )
    rank_reduced = lax.psum(partial_value, "tensor").astype(jnp.bfloat16)
    block_count = block_rows.shape[0]
    base_terms = jnp.dot(
        block_rows.reshape(block_count * queued_block_rows, width_dev),
        key_value_weight,
        preferred_element_type=jnp.float32,
    )
    base_key_value = lax.psum_scatter(base_terms, "tensor", scatter_dimension=1, tiled=True)
    output_columns = base_key_value.shape[1]
    adapter_delta = jnp.einsum(
        "abq,abp->aqp", rank_reduced, up_slices, preferred_element_type=jnp.float32
    )
    projected_output = (
        base_key_value.reshape(block_count, queued_block_rows, output_columns)
        + adapter_scale * adapter_delta
    ).astype(jnp.bfloat16)
    return projected_output.reshape(replica_slot_count * queued_block_rows, output_columns)


def solution(mesh):
    return jax.shard_map(
        shards,
        mesh=mesh,
        in_specs=(
            P(("groups", "replica"), "tensor"),
            P(("groups", "replica")),
            P("groups", None),
            P("tensor", None),
            P(("groups", "replica"), None, "tensor"),
            P(("groups", "replica"), None, "tensor"),
        ),
        out_specs=P(("groups", "replica"), "tensor"),
        check_vma=False,
    )
```
